32 devices in a mesh: dom: 4 (over y, core), mem: 8 (over z, x).
Axes of the slice: x: 2, y: 2, z: 4, core: 2. Of those that a mesh axis runs over, the one named last changes fastest.
Arguments:
- control: bfloat16 [64, 128, 8192], P('mem', None, 'dom'), may hold values from -6 to 6
- corr_offsets: int32 [64, 4], P('dom'), may hold values from -2 to 2, as said below
- corr_blocks: bfloat16 [64, 4, 128, 128], P('dom'), may hold values from -0.25 to 0.25
- interp_index: int32 [64, 4], P('dom'), may hold values from 0 to 15
- interp_blocks: bfloat16 [64, 4, 128, 128], P('dom'), may hold values from -0.25 to 0.25
- perturbations: bfloat16 [64, 128, 8192], P('mem', None, 'dom'), may hold values from -6 to 6
Outputs:
- increment: bfloat16 [128, 8192], P(None, 'dom')
The draws below stay inside these ranges and needn't reach their ends.
Inputs may be any that keep to these rules, and one draw needn't show every extreme that they name: `corr_offsets`: each row holds 4 distinct offsets, among them 0, -2 and 2; exactly one of -1 and 1 is absent from each row. `interp_index`: an entry names a subgrid block of the tile that owns the column block, counted from that tile's first block.
All inputs are finite; a program needn't handle non-finite values.
Results may differ from the reference program's by a relative error of at most 0.0049.
Values may be sent and summed in bfloat16 or wider, within the bound.
A program may use at most 128 MiB of HBM per device.

```python
import jax
import jax.numpy as jnp
import numpy as np
from jax import lax

BLK = 128
HR = 2
NI = 4
LEV = 128
SB_DEV = 16
COLB_DEV = 16
NNZ = 4
MEMBERS = 64
NBLK = 64
SUB = 8192
NCOLB = 64
COLS = 8192


def draw_corr_offsets(key, part):
    without_low = np.array([shift for shift in range(-HR, HR + 1) if shift != -1], np.int32)
    without_high = np.array([shift for shift in range(-HR, HR + 1) if shift != 1], np.int32)
    first_key, second_key = jax.random.split(jax.random.fold_in(key, 11))
    choose = jax.random.randint(first_key, (NBLK, 1), 0, 2)
    kept = jnp.where(choose == 0, jnp.asarray(without_low)[None, :], jnp.asarray(without_high)[None, :])
    scores = jax.random.randint(second_key, (NBLK, NNZ), 0, 1 << 20) * NNZ + jnp.arange(NNZ, dtype=jnp.int32)[None, :]
    arrangement = jnp.argsort(scores, axis=1)
    return jnp.take_along_axis(kept, arrangement, axis=1).astype(jnp.int32)


def set_ends(values, rng, smallest, high):
    index_at = [jax.random.randint(jax.random.fold_in(rng, axis), (), 0, length) for axis, length in enumerate(values.shape)]
    widest = values.shape.index(max(values.shape))
    neighbour = index_at[:widest] + [(index_at[widest] + 1) % values.shape[widest]] + index_at[widest + 1:]
    return values.at[tuple(index_at)].set(smallest).at[tuple(neighbour)].set(high)


def with_spikes(values, stream_key, source, target, shards_of, factor):
    owner, partner = [(jnp.arange(values.shape[dim]) // (values.shape[dim] // shards_of)).reshape([-1 if axis == dim else 1 for axis in range(values.ndim)]) for dim in (source, target)]
    chosen = jax.random.permutation(stream_key, shards_of)[partner]
    strong = (owner == chosen) | (owner == (partner + shards_of // 2) % shards_of)
    return jnp.where(strong, factor * values, values)


def steps_of(own_key, shape, shards, low, largest):
    def one(dim, blocks):
        steps = jax.random.uniform(jax.random.fold_in(jax.random.fold_in(own_key, 6), dim), (blocks,), jnp.float32, low / len(shards), largest / len(shards))
        return jnp.repeat(jnp.exp(steps), shape[dim] // blocks).reshape((-1,) + (1,) * (len(shape) - dim - 1))

    loudness = one(*shards[0])
    for cut in shards[1:]:
        loudness = loudness * one(*cut)
    return loudness


def bell_draw(rng, extent, scale, limit, pieces=(), kind=jnp.bfloat16):
    entries = jax.random.normal(rng, extent, jnp.float32) * scale
    if len(pieces) > 0:
        entries = steps_of(rng, extent, pieces, -0.22, 0.18) * entries
    return jnp.clip(entries, min=-limit, max=limit).astype(kind)


def gaussian_with(stream_key, dims, deviation, bound, shards, heavy, kind=jnp.bfloat16):
    result = deviation * jax.random.normal(stream_key, dims, jnp.float32)
    if shards:
        result = result * steps_of(stream_key, dims, shards, -0.22, 0.18)
    return jnp.clip(with_spikes(result, jax.random.fold_in(stream_key, 3), *heavy), -bound, bound).astype(kind)


def setup_inputs(seed: int = 0) -> dict:
    streams_of = jax.random.split(jax.random.key(seed), 7)
    return {
        "control": bell_draw(streams_of[0], (MEMBERS, LEV, SUB), 1.0, 6.0, ((0, 8), (2, 4))),
        "corr_offsets": draw_corr_offsets(jax.random.fold_in(streams_of[6], 71), 0),
        "corr_blocks": bell_draw(streams_of[2], (NBLK, NNZ, BLK, BLK), (NNZ * BLK) ** -0.5, 0.25, ((0, 4),)),
        "interp_index": set_ends(jax.random.randint(streams_of[3], (NCOLB, NI), 0, SB_DEV), jax.random.fold_in(streams_of[3], 1), 0, SB_DEV - 1).astype(jnp.int32),
        "interp_blocks": bell_draw(streams_of[4], (NCOLB, NI, BLK, BLK), (NI * BLK) ** -0.5, 0.25, ((0, 4),)),
        "perturbations": gaussian_with(streams_of[5], (MEMBERS, LEV, COLS), 1.0, 6.0, ((0, 8), (2, 4)), (0, 1, 8, 2.0)),
    }


def reference(control, corr_offsets, corr_blocks, interp_index, interp_blocks, perturbations):
    blocks_all = corr_blocks.shape[0]
    breadth = corr_blocks.shape[2]
    column_blocks = interp_blocks.shape[0]
    levels = control.shape[1]
    source = (jnp.arange(blocks_all, dtype=jnp.int32)[:, None] + corr_offsets.astype(jnp.int32)) % blocks_all
    owner_tile = jnp.arange(column_blocks, dtype=jnp.int32) // COLB_DEV
    feeding = owner_tile[:, None] * SB_DEV + interp_index.astype(jnp.int32)
    corr_wide = corr_blocks.astype(jnp.float32)
    interp_wide = interp_blocks.astype(jnp.float32)

    def one_member(summed, paired):
        member_control, member_pert = paired
        tiled = member_control.astype(jnp.float32).reshape(levels, blocks_all, breadth)
        smoothed = jnp.einsum('lbsj,bsji->lbi', tiled[:, source], corr_wide, precision=lax.Precision.HIGHEST)
        smoothed = smoothed.astype(jnp.bfloat16).astype(jnp.float32)
        spread = jnp.einsum('lqkj,qkji->lqi', smoothed[:, feeding], interp_wide, precision=lax.Precision.HIGHEST)
        updated = summed + member_pert.astype(jnp.float32) * spread.reshape(levels, column_blocks * breadth)
        return (updated, None)
    initial = jnp.zeros((levels, column_blocks * breadth), jnp.float32)
    summed = lax.scan(one_member, initial, (control, perturbations))[0]
    factor = 1.0 / jnp.sqrt(jnp.float32(MEMBERS - 1))
    return (summed * factor).astype(jnp.bfloat16)
```

```python
import functools

import jax
import jax.numpy as jnp
from jax import lax
from jax.experimental import pallas as pl
from jax.experimental.pallas import tpu as pltpu
from jax.sharding import PartitionSpec as P

HR = 2
MESH = pl.DeviceIdType.MESH
RATE = 2


def chunk_sizes(levels):
    size = 32 if levels % 32 == 0 else levels
    return [size] * (levels // size)


def kernel(
    sizes, doms, mems,
    offs_ref, index_ref, control_ref, corr_ref, interp_ref, pert_ref,
    out_ref,
    *scratch,
):
    count = len(sizes)
    starts = [sum(sizes[:c]) for c in range(count)]
    bits = mems.bit_length() - 1
    halvings = bits - 1
    scratch = list(scratch)

    def take(n):
        got = scratch[:n]
        del scratch[:n]
        return got

    exts, smooths, perts = take(count), take(count), take(count)
    corr_v, interp_v, wide = take(3)
    txs = [take(bits) for _ in range(count)]
    rxs = [take(bits) for _ in range(count)]
    owns = [take(halvings) for _ in range(count)]
    load_sem, halo_send, halo_recv, red_send, red_recv, gat_send, gat_recv = take(7)

    members = control_ref.shape[0]
    blocks, stored, breadth = corr_ref.shape[0], corr_ref.shape[1], corr_ref.shape[2]
    column_blocks, feeds = interp_ref.shape[0], interp_ref.shape[1]
    width = blocks * breadth
    edge = HR * breadth
    pairs = blocks // 2

    me_dom = lax.axis_index("dom")
    me = lax.axis_index("mem")
    right = lax.rem(me_dom + 1, doms)
    left = lax.rem(me_dom + doms - 1, doms)
    bit = [lax.rem(me // (1 << s), 2) for s in range(bits)]
    partner = [me + (1 - 2 * bit[s]) * (1 << s) for s in range(bits)]

    def loaded(src, dst, slot):
        copy = pltpu.make_async_copy(src, dst, load_sem.at[slot])
        copy.start()
        return copy

    corr_load = loaded(corr_ref, corr_v, 0)
    control_loads = [
        loaded(
            control_ref.at[:, pl.ds(starts[c], sizes[c]), :],
            exts[c].at[:, :, pl.ds(edge, width)],
            2 + c,
        )
        for c in range(count)
    ]
    interp_load = loaded(interp_ref, interp_v, 1)
    pert_loads = [
        loaded(pert_ref.at[:, pl.ds(starts[c], sizes[c]), :], perts[c], 2 + count + c)
        for c in range(count)
    ]

    barrier = pltpu.get_barrier_semaphore()
    for neighbour in (left, right):
        pl.semaphore_signal(barrier, inc=1, device_id={"dom": neighbour}, device_id_type=MESH)
    for s in range(bits):
        pl.semaphore_signal(barrier, inc=1, device_id={"mem": partner[s]}, device_id_type=MESH)
    pl.semaphore_wait(barrier, 2 + bits)

    halos = []
    for c in range(count):
        rows = pl.ds(starts[c], sizes[c])
        pair = []
        for side, (src, dst, to) in enumerate(
            ((width - edge, 0, right), (0, edge + width, left))
        ):
            copy = pltpu.make_async_remote_copy(
                src_ref=control_ref.at[:, rows, pl.ds(src, edge)],
                dst_ref=exts[c].at[:, :, pl.ds(dst, edge)],
                send_sem=halo_send.at[2 * c + side],
                recv_sem=halo_recv.at[2 * c + side],
                device_id={"dom": to},
                device_id_type=MESH,
            )
            copy.start()
            pair.append(copy)
        halos.append(pair)

    corr_load.wait()

    def widen(p, carry):
        for r in range(2):
            b = 2 * p + r
            for j in range(2 + 2 * HR):
                shift = j - HR - r
                cell = (
                    p,
                    pl.ds(j * breadth, breadth),
                    pl.ds(r * breadth, breadth),
                )
                if abs(shift) > HR:
                    wide[cell] = jnp.zeros((breadth, breadth), wide.dtype)
                    continue
                slot = jnp.int32(0)
                found = jnp.int32(0)
                for s in range(stored):
                    here = offs_ref[s, b] == shift
                    slot = jnp.where(here, s, slot)
                    found = jnp.where(here, 1, found)
                value = corr_v[b, slot]
                if abs(shift) == 1:
                    value = value * found.astype(jnp.float32).astype(value.dtype)
                wide[cell] = value
        return carry

    lax.fori_loop(0, pairs, widen, 0)

    def smooth(c, p):
        rows = members * sizes[c]
        lhs = exts[c][:, :, pl.ds(pl.multiple_of(2 * p * breadth, breadth), (2 + 2 * HR) * breadth)]
        got = jnp.dot(
            lhs.reshape(rows, (2 + 2 * HR) * breadth), wide[p], preferred_element_type=jnp.float32
        ).astype(smooths[c].dtype)
        smooths[c][2 * p] = got[:, :breadth]
        smooths[c][2 * p + 1] = got[:, breadth:]

    for c in range(count):
        control_loads[c].wait()

        def inner(p, carry, c=c):
            smooth(c, p)
            return carry

        lax.fori_loop(1, pairs - 1, inner, 0, unroll=2)

    def columns(c, q):
        rows = members * sizes[c]
        lhs = jnp.concatenate(
            [smooths[c][index_ref[k, q]] for k in range(feeds)], axis=1
        )
        rhs = interp_v[q].reshape(feeds * breadth, breadth)
        spread = jnp.dot(lhs, rhs, preferred_element_type=jnp.float32)
        spread = spread.reshape(members, sizes[c], breadth)
        at = pl.ds(pl.multiple_of(q * breadth, breadth), breadth)
        return jnp.sum(perts[c][:, :, at].astype(jnp.float32) * spread, axis=0)

    def exchange(c, s):
        copy = pltpu.make_async_remote_copy(
            src_ref=txs[c][s],
            dst_ref=rxs[c][s],
            send_sem=red_send.at[c * bits + s],
            recv_sem=red_recv.at[c * bits + s],
            device_id={"mem": partner[s]},
            device_id_type=MESH,
        )
        copy.start()
        return copy

    half = [column_blocks >> (s + 1) for s in range(halvings)]
    held = [sum((bit[t] * half[t] for t in range(s + 1)), jnp.int32(0)) for s in range(halvings)]
    factor = 1.0 / jnp.sqrt(jnp.float32(members * mems - 1))
    reduces, gathers = {}, {}

    def compute(c):
        for copy in halos[c]:
            copy.wait_recv()
        if c == 0:
            interp_load.wait()
        pert_loads[c].wait()
        smooth(c, 0)
        smooth(c, pairs - 1)

        def away(j, carry):
            txs[c][0][j] = columns(c, (1 - bit[0]) * half[0] + j).astype(jnp.bfloat16)
            return carry

        def kept(j, carry):
            owns[c][0][j] = columns(c, bit[0] * half[0] + j)
            return carry

        lax.fori_loop(0, half[0], away, 0, unroll=2)
        reduces[c, 0] = exchange(c, 0)
        lax.fori_loop(0, half[0], kept, 0, unroll=2)

    def gather(c, s):
        place = out_ref.at[
            pl.ds(starts[c], sizes[c]),
            pl.ds(pl.multiple_of(held[s] * breadth, breadth), half[s] * breadth),
        ]
        copy = pltpu.make_async_remote_copy(
            src_ref=place,
            dst_ref=place,
            send_sem=gat_send.at[c * halvings + s],
            recv_sem=gat_recv.at[c * halvings + s],
            device_id={"mem": partner[s]},
            device_id_type=MESH,
        )
        copy.start()
        return copy

    def advance(c, stage):
        if stage < bits:
            reduces[c, stage].wait_recv()
        if stage < halvings - 1:
            size = half[stage + 1]
            send, keep = (1 - bit[stage + 1]) * size, bit[stage + 1] * size
            for i in range(size):
                txs[c][stage + 1][i] = (
                    owns[c][stage][send + i] + rxs[c][stage][send + i].astype(jnp.float32)
                ).astype(jnp.bfloat16)
            reduces[c, stage + 1] = exchange(c, stage + 1)
            for i in range(size):
                owns[c][stage + 1][i] = owns[c][stage][keep + i] + rxs[c][stage][
                    keep + i
                ].astype(jnp.float32)
        elif stage == halvings - 1:
            for i in range(half[stage]):
                txs[c][stage + 1][i] = (
                    owns[c][stage][i] + rxs[c][stage][i].astype(jnp.float32)
                ).astype(jnp.bfloat16)
            reduces[c, stage + 1] = exchange(c, stage + 1)
        elif stage == halvings:
            for i in range(half[-1]):
                total = txs[c][stage][i].astype(jnp.float32) + rxs[c][stage][i].astype(jnp.float32)
                at = pl.ds(pl.multiple_of((held[-1] + i) * breadth, breadth), breadth)
                out_ref[pl.ds(starts[c], sizes[c]), at] = (total * factor).astype(out_ref.dtype)
            gathers[c, halvings - 1] = gather(c, halvings - 1)
        else:
            s = 2 * halvings - stage
            gathers[c, s].wait_recv()
            if s > 0:
                gathers[c, s - 1] = gather(c, s - 1)

    steps = []
    for c in range(count):
        steps.append((RATE * c, 0, c, None))
        for stage in range(2 * halvings + 1):
            steps.append((RATE * (c + 1) + stage, 1, c, stage))
    for _, kind, c, stage in sorted(steps, key=lambda step: step[:3]):
        if kind == 0:
            compute(c)
        else:
            advance(c, stage)

    for pair in halos:
        for copy in pair:
            copy.wait_send()
    for key in sorted(reduces):
        reduces[key].wait_send()
    for key in sorted(gathers):
        gathers[key].wait_send()


def per_device(doms, mems, control, corr_offsets, corr_blocks, interp_index, interp_blocks, perturbations):
    members, levels, width = control.shape
    blocks, _, breadth, _ = corr_blocks.shape
    column_blocks = interp_blocks.shape[0]
    sizes = chunk_sizes(levels)
    count = len(sizes)
    bits = mems.bit_length() - 1
    halvings = bits - 1
    bf16, f32 = jnp.bfloat16, jnp.float32
    half = [column_blocks >> (s + 1) for s in range(halvings)]
    moved = half + [half[-1]]
    scratch = []
    scratch += [pltpu.VMEM((members, n, width + 2 * HR * breadth), bf16) for n in sizes]
    scratch += [pltpu.VMEM((blocks, members * n, breadth), bf16) for n in sizes]
    scratch += [pltpu.VMEM((members, n, perturbations.shape[2]), bf16) for n in sizes]
    scratch += [
        pltpu.VMEM(corr_blocks.shape, bf16),
        pltpu.VMEM(interp_blocks.shape, bf16),
        pltpu.VMEM((blocks // 2, (2 + 2 * HR) * breadth, 2 * breadth), bf16),
    ]
    for _ in range(2):
        scratch += [pltpu.VMEM((h, n, breadth), bf16) for n in sizes for h in moved]
    scratch += [pltpu.VMEM((h, n, breadth), f32) for n in sizes for h in half]
    scratch += [
        pltpu.SemaphoreType.DMA((2 + 2 * count,)),
        pltpu.SemaphoreType.DMA((2 * count,)),
        pltpu.SemaphoreType.DMA((2 * count,)),
        pltpu.SemaphoreType.DMA((count * bits,)),
        pltpu.SemaphoreType.DMA((count * bits,)),
        pltpu.SemaphoreType.DMA((count * halvings,)),
        pltpu.SemaphoreType.DMA((count * halvings,)),
    ]
    hbm = pl.BlockSpec(memory_space=pl.ANY)
    smem = pl.BlockSpec(memory_space=pltpu.SMEM)
    flops = 2 * members * levels * breadth * breadth * (6 * blocks + 4 * column_blocks)
    return pl.pallas_call(
        functools.partial(kernel, sizes, doms, mems),
        out_shape=jax.ShapeDtypeStruct((levels, column_blocks * breadth), bf16),
        in_specs=[smem, smem, hbm, hbm, hbm, hbm],
        out_specs=pl.BlockSpec(memory_space=pltpu.VMEM),
        scratch_shapes=scratch,
        compiler_params=pltpu.CompilerParams(
            collective_id=0, has_side_effects=True, vmem_limit_bytes=56 << 20
        ),
        cost_estimate=pl.CostEstimate(flops=flops, bytes_accessed=13 << 20, transcendentals=0),
    )(corr_offsets.T, interp_index.T, control, corr_blocks, interp_blocks, perturbations)


def solution(mesh):
    in_specs = (
        P("mem", None, "dom"),
        P("dom", None),
        P("dom", None, None, None),
        P("dom", None),
        P("dom", None, None, None),
        P("mem", None, "dom"),
    )
    out_specs = P(None, "dom")
    return jax.shard_map(
        functools.partial(per_device, mesh.shape["dom"], mesh.shape["mem"]),
        mesh=mesh, in_specs=in_specs, out_specs=out_specs, check_vma=False,
    )
```

```python
import functools

import jax
import jax.numpy as jnp
from jax import lax
from jax.experimental import pallas as pl
from jax.experimental.pallas import tpu as pltpu
from jax.sharding import PartitionSpec as P

HR = 2
MESH = pl.DeviceIdType.MESH
SIDE = 4


def chunk_sizes(levels):
    if levels % 32:
        return [levels]
    return [32] * (levels // 32 - 1) + [16, 16]


def kernel(
    sizes, doms, mems,
    offs_ref, index_ref, control_ref, corr_ref, interp_ref, pert_ref,
    out_ref,
    *scratch,
):
    count = len(sizes)
    starts = [sum(sizes[:c]) for c in range(count)]
    bits = mems.bit_length() - 1
    later = bits - 2
    peers = (3, 2, 1)
    scratch = list(scratch)

    def take(n):
        got = scratch[:n]
        del scratch[:n]
        return got

    exts, smooths, perts = take(count), take(count), take(count)
    corr_v, interp_v, wide = take(3)
    txs = [take(len(peers)) for _ in range(count)]
    rxs = [take(len(peers)) for _ in range(count)]
    sums_tx = [take(later) for _ in range(count)]
    sums_rx = [take(later) for _ in range(count)]
    owns, finals = take(count), take(count)
    load_sem, store_sem, halo_send, halo_recv = take(4)
    red_send, red_recv, sum_send, sum_recv, gat_send, gat_recv = take(6)

    members = control_ref.shape[0]
    blocks, stored, breadth = corr_ref.shape[0], corr_ref.shape[1], corr_ref.shape[2]
    column_blocks, feeds = interp_ref.shape[0], interp_ref.shape[1]
    width = blocks * breadth
    edge = HR * breadth
    pairs = blocks // 2

    me_dom = lax.axis_index("dom")
    me = lax.axis_index("mem")
    right = lax.rem(me_dom + 1, doms)
    left = lax.rem(me_dom + doms - 1, doms)
    bit = [lax.rem(me // (1 << s), 2) for s in range(bits)]

    def flipped(t):
        return me + sum((1 - 2 * bit[s]) * (1 << s) for s in range(bits) if (t >> s) & 1)

    def quarter(t):
        return lax.rem(flipped(t), SIDE) if t else lax.rem(me, SIDE)

    met = list(peers) + [1 << s for s in range(2, bits)]

    def loaded(src, dst, slot):
        copy = pltpu.make_async_copy(src, dst, load_sem.at[slot])
        copy.start()
        return copy

    corr_load = loaded(corr_ref, corr_v, 0)
    control_loads = [
        loaded(
            control_ref.at[:, pl.ds(starts[c], sizes[c]), :],
            exts[c].at[:, :, pl.ds(edge, width)],
            2 + c,
        )
        for c in range(count)
    ]
    interp_load = loaded(interp_ref, interp_v, 1)
    pert_loads = [
        loaded(pert_ref.at[:, pl.ds(starts[c], sizes[c]), :], perts[c], 2 + count + c)
        for c in range(count)
    ]

    barrier = pltpu.get_barrier_semaphore()
    for neighbour in (left, right):
        pl.semaphore_signal(barrier, inc=1, device_id={"dom": neighbour}, device_id_type=MESH)
    for t in met:
        pl.semaphore_signal(barrier, inc=1, device_id={"mem": flipped(t)}, device_id_type=MESH)
    pl.semaphore_wait(barrier, 2 + len(met))

    halos = []

    def send_halo():
        c = len(halos)
        if c == count:
            return
        rows = pl.ds(starts[c], sizes[c])
        pair = []
        for side, (src, dst, to) in enumerate(
            ((width - edge, 0, right), (0, edge + width, left))
        ):
            copy = pltpu.make_async_remote_copy(
                src_ref=control_ref.at[:, rows, pl.ds(src, edge)],
                dst_ref=exts[c].at[:, :, pl.ds(dst, edge)],
                send_sem=halo_send.at[2 * c + side],
                recv_sem=halo_recv.at[2 * c + side],
                device_id={"dom": to},
                device_id_type=MESH,
            )
            copy.start()
            pair.append(copy)
        halos.append(pair)

    def halo_left(c):
        for copy in halos[c]:
            copy.wait_send()

    send_halo()

    corr_load.wait()

    def widen(p, carry):
        for r in range(2):
            b = 2 * p + r
            for j in range(2 + 2 * HR):
                shift = j - HR - r
                cell = (
                    p,
                    pl.ds(j * breadth, breadth),
                    pl.ds(r * breadth, breadth),
                )
                if abs(shift) > HR:
                    wide[cell] = jnp.zeros((breadth, breadth), wide.dtype)
                    continue
                slot = jnp.int32(0)
                found = jnp.int32(0)
                for s in range(stored):
                    here = offs_ref[s, b] == shift
                    slot = jnp.where(here, s, slot)
                    found = jnp.where(here, 1, found)
                value = corr_v[b, slot]
                if abs(shift) == 1:
                    value = value * found.astype(jnp.float32).astype(value.dtype)
                wide[cell] = value
        return carry

    lax.fori_loop(0, pairs, widen, 0)
    send_halo()

    def smooth(c, p):
        rows = members * sizes[c]
        lhs = exts[c][:, :, pl.ds(pl.multiple_of(2 * p * breadth, breadth), (2 + 2 * HR) * breadth)]
        got = jnp.dot(
            lhs.reshape(rows, (2 + 2 * HR) * breadth), wide[p], preferred_element_type=jnp.float32
        ).astype(smooths[c].dtype)
        smooths[c][2 * p] = got[:, :breadth]
        smooths[c][2 * p + 1] = got[:, breadth:]

    for c in range(count):
        control_loads[c].wait()

        def inner(p, carry, c=c):
            smooth(c, p)
            return carry

        lax.fori_loop(1, pairs - 1, inner, 0, unroll=3)

    def columns(c, q):
        rows = members * sizes[c]
        lhs = jnp.concatenate(
            [smooths[c][index_ref[k, q]] for k in range(feeds)], axis=1
        )
        rhs = interp_v[q].reshape(feeds * breadth, breadth)
        spread = jnp.dot(lhs, rhs, preferred_element_type=jnp.float32)
        spread = spread.reshape(members, sizes[c], breadth)
        at = pl.ds(pl.multiple_of(q * breadth, breadth), breadth)
        return jnp.sum(perts[c][:, :, at].astype(jnp.float32) * spread, axis=0)

    def remote(src, dst, send, recv, t):
        copy = pltpu.make_async_remote_copy(
            src_ref=src, dst_ref=dst, send_sem=send, recv_sem=recv,
            device_id={"mem": flipped(t)}, device_id_type=MESH,
        )
        copy.start()
        return copy

    share = column_blocks // SIDE
    factor = 1.0 / jnp.sqrt(jnp.float32(members * mems - 1))
    reduces, exchanges, gathers, stores = {}, {}, {}, []

    def compute(c):
        for copy in halos[c]:
            copy.wait_recv()
        if c == 0:
            interp_load.wait()
        pert_loads[c].wait()
        smooth(c, 0)
        smooth(c, pairs - 1)
        if len(halos) < count:
            halo_left(c)
            send_halo()
        for n, t in enumerate(peers):
            def away(j, carry, n=n, t=t):
                txs[c][n][j] = columns(c, quarter(t) * share + j).astype(jnp.bfloat16)
                return carry

            lax.fori_loop(0, share, away, 0, unroll=True)
            at = c * len(peers) + n
            reduces[c, n] = remote(txs[c][n], rxs[c][n], red_send.at[at], red_recv.at[at], t)

        def kept(j, carry):
            owns[c][j] = columns(c, quarter(0) * share + j)
            return carry

        lax.fori_loop(0, share, kept, 0, unroll=True)

    def finish(c, j, total):
        at = pl.ds(j * breadth, breadth)
        finals[c][:, at] = (total * factor).astype(out_ref.dtype)

    def advance(c, stage):
        if stage == 0:
            for n in range(len(peers)):
                reduces[c, n].wait_recv()
        else:
            exchanges[c, stage - 1].wait_recv()
        for j in range(share):
            if stage == 0:
                total = owns[c][j]
                for n in range(len(peers)):
                    total = total + rxs[c][n][j].astype(jnp.float32)
            else:
                total = sums_tx[c][stage - 1][j].astype(jnp.float32) + sums_rx[c][stage - 1][
                    j
                ].astype(jnp.float32)
            if stage < later:
                sums_tx[c][stage][j] = total.astype(jnp.bfloat16)
            else:
                finish(c, j, total)
        if stage < later:
            at = c * later + stage
            exchanges[c, stage] = remote(
                sums_tx[c][stage], sums_rx[c][stage], sum_send.at[at], sum_recv.at[at], 1 << (stage + 2)
            )
            return
        place = out_ref.at[
            pl.ds(starts[c], sizes[c]),
            pl.ds(pl.multiple_of(quarter(0) * (share * breadth), breadth), share * breadth),
        ]
        for n, t in enumerate(peers):
            at = c * len(peers) + n
            gathers[c, n] = remote(finals[c], place, gat_send.at[at], gat_recv.at[at], t)
        store = pltpu.make_async_copy(finals[c], place, store_sem.at[c])
        store.start()
        stores.append(store)

    steps = [(c, 0, c, None) for c in range(count)]
    steps += [(c + 1 + stage, 1, c, stage) for c in range(count) for stage in range(later + 1)]
    for _, kind, c, stage in sorted(steps, key=lambda step: step[:3]):
        if kind == 0:
            compute(c)
        else:
            advance(c, stage)

    for c in range(max(count - 2, 0), count):
        halo_left(c)
    for group in (reduces, exchanges):
        for key in sorted(group):
            group[key].wait_send()
    for key in sorted(gathers):
        gathers[key].wait()
    for store in stores:
        store.wait()


def per_device(doms, mems, control, corr_offsets, corr_blocks, interp_index, interp_blocks, perturbations):
    members, levels, width = control.shape
    blocks, _, breadth, _ = corr_blocks.shape
    column_blocks = interp_blocks.shape[0]
    sizes = chunk_sizes(levels)
    count = len(sizes)
    later = mems.bit_length() - 3
    share = column_blocks // SIDE
    bf16, f32 = jnp.bfloat16, jnp.float32
    scratch = []
    scratch += [pltpu.VMEM((members, n, width + 2 * HR * breadth), bf16) for n in sizes]
    scratch += [pltpu.VMEM((blocks, members * n, breadth), bf16) for n in sizes]
    scratch += [pltpu.VMEM((members, n, perturbations.shape[2]), bf16) for n in sizes]
    scratch += [
        pltpu.VMEM(corr_blocks.shape, bf16),
        pltpu.VMEM(interp_blocks.shape, bf16),
        pltpu.VMEM((blocks // 2, (2 + 2 * HR) * breadth, 2 * breadth), bf16),
    ]
    for times in (SIDE - 1, SIDE - 1, later, later):
        scratch += [pltpu.VMEM((share, n, breadth), bf16) for n in sizes for _ in range(times)]
    scratch += [pltpu.VMEM((share, n, breadth), f32) for n in sizes]
    scratch += [pltpu.VMEM((n, share * breadth), bf16) for n in sizes]
    scratch += [
        pltpu.SemaphoreType.DMA((n,))
        for n in (2 + 2 * count, count, 2 * count, 2 * count, 3 * count, 3 * count)
        + (later * count, later * count, 3 * count, 3 * count)
    ]
    hbm = pl.BlockSpec(memory_space=pl.ANY)
    smem = pl.BlockSpec(memory_space=pltpu.SMEM)
    flops = 2 * members * levels * breadth * breadth * (6 * blocks + 4 * column_blocks)
    return pl.pallas_call(
        functools.partial(kernel, sizes, doms, mems),
        out_shape=jax.ShapeDtypeStruct((levels, column_blocks * breadth), bf16),
        in_specs=[smem, smem, hbm, hbm, hbm, hbm],
        out_specs=hbm,
        scratch_shapes=scratch,
        compiler_params=pltpu.CompilerParams(
            collective_id=0, has_side_effects=True, vmem_limit_bytes=56 << 20
        ),
        cost_estimate=pl.CostEstimate(flops=flops, bytes_accessed=13 << 20, transcendentals=0),
    )(corr_offsets.T, interp_index.T, control, corr_blocks, interp_blocks, perturbations)


def solution(mesh):
    in_specs = (
        P("mem", None, "dom"),
        P("dom", None),
        P("dom", None, None, None),
        P("dom", None),
        P("dom", None, None, None),
        P("mem", None, "dom"),
    )
    out_specs = P(None, "dom")
    return jax.shard_map(
        functools.partial(per_device, mesh.shape["dom"], mesh.shape["mem"]),
        mesh=mesh, in_specs=in_specs, out_specs=out_specs, check_vma=False,
    )
```

```python
import functools

import jax
import jax.numpy as jnp
from jax import lax
from jax.experimental import pallas as pl
from jax.experimental.pallas import tpu as pltpu
from jax.sharding import PartitionSpec as P

HR = 2
MESH = pl.DeviceIdType.MESH
SIDE = 4


def chunk_sizes(levels):
    if levels % 64:
        return [levels]
    return [levels // 2] + [32] * (levels // 64)


def kernel(
    sizes, doms, mems,
    offs_ref, index_ref, control_ref, corr_ref, interp_ref, pert_ref,
    out_ref,
    *scratch,
):
    count = len(sizes)
    starts = [sum(sizes[:c]) for c in range(count)]
    bits = mems.bit_length() - 1
    later = bits - 2
    peers = (3, 2, 1)
    scratch = list(scratch)

    def take(n):
        got = scratch[:n]
        del scratch[:n]
        return got

    perts = take(count)
    ext, smoothed, corr_v, interp_v, wide = take(5)
    txs, rxs = take(count), take(count)
    sums_tx = [take(later) for _ in range(count)]
    sums_rx = [take(later) for _ in range(count)]
    owns, finals = take(count), take(count)
    load_sem, store_sem, halo_send, halo_recv = take(4)
    red_send, red_recv, sum_send, sum_recv, gat_send, gat_recv = take(6)

    members = control_ref.shape[0]
    blocks, stored, breadth = corr_ref.shape[0], corr_ref.shape[1], corr_ref.shape[2]
    column_blocks, feeds = interp_ref.shape[0], interp_ref.shape[1]
    width = blocks * breadth
    edge = HR * breadth
    pairs = blocks // 2

    me_dom = lax.axis_index("dom")
    me = lax.axis_index("mem")
    right = lax.rem(me_dom + 1, doms)
    left = lax.rem(me_dom + doms - 1, doms)
    bit = [lax.rem(me // (1 << s), 2) for s in range(bits)]

    def flipped(t):
        return me + sum((1 - 2 * bit[s]) * (1 << s) for s in range(bits) if (t >> s) & 1)

    def quarter(t):
        return lax.rem(flipped(t), SIDE) if t else lax.rem(me, SIDE)

    met = list(peers) + [1 << s for s in range(2, bits)]

    def loaded(src, dst, slot):
        copy = pltpu.make_async_copy(src, dst, load_sem.at[slot])
        copy.start()
        return copy

    corr_load = loaded(corr_ref, corr_v, 0)
    portion = control_ref.shape[1] // 2
    control_loads = [
        loaded(
            control_ref.at[:, pl.ds(h * portion, portion), :],
            ext.at[:, pl.ds(h * portion, portion), pl.ds(edge, width)],
            2 + h,
        )
        for h in range(2)
    ]
    interp_load = loaded(interp_ref, interp_v, 1)
    pert_loads = [
        loaded(pert_ref.at[:, pl.ds(starts[c], sizes[c]), :], perts[c], 4 + c)
        for c in range(count)
    ]

    barrier = pltpu.get_barrier_semaphore()
    for neighbour in (left, right):
        pl.semaphore_signal(barrier, inc=1, device_id={"dom": neighbour}, device_id_type=MESH)
    for t in met:
        pl.semaphore_signal(barrier, inc=1, device_id={"mem": flipped(t)}, device_id_type=MESH)
    pl.semaphore_wait(barrier, 2 + len(met))

    halos = []

    def send_halo():
        c = len(halos)
        if c == count:
            return
        rows = pl.ds(starts[c], sizes[c])
        pair = []
        for side, (src, dst, to) in enumerate(
            ((width - edge, 0, right), (0, edge + width, left))
        ):
            copy = pltpu.make_async_remote_copy(
                src_ref=control_ref.at[:, rows, pl.ds(src, edge)],
                dst_ref=ext.at[:, rows, pl.ds(dst, edge)],
                send_sem=halo_send.at[2 * c + side],
                recv_sem=halo_recv.at[2 * c + side],
                device_id={"dom": to},
                device_id_type=MESH,
            )
            copy.start()
            pair.append(copy)
        halos.append(pair)

    def halo_left(c):
        for copy in halos[c]:
            copy.wait_send()

    send_halo()

    corr_load.wait()

    def widen(p, carry):
        for r in range(2):
            b = 2 * p + r
            for j in range(2 + 2 * HR):
                shift = j - HR - r
                cell = (
                    p,
                    pl.ds(j * breadth, breadth),
                    pl.ds(r * breadth, breadth),
                )
                if abs(shift) > HR:
                    wide[cell] = jnp.zeros((breadth, breadth), wide.dtype)
                    continue
                slot = jnp.int32(0)
                found = jnp.int32(0)
                for s in range(stored):
                    here = offs_ref[s, b] == shift
                    slot = jnp.where(here, s, slot)
                    found = jnp.where(here, 1, found)
                value = corr_v[b, slot]
                if abs(shift) == 1:
                    value = value * found.astype(jnp.float32).astype(value.dtype)
                wide[cell] = value
        return carry

    lax.fori_loop(0, pairs, widen, 0)
    send_halo()

    def smooth(start, size, p):
        rows = pl.ds(start, size)
        across = pl.ds(pl.multiple_of(2 * p * breadth, breadth), (2 + 2 * HR) * breadth)
        lhs = ext[:, rows, across].reshape(members * size, (2 + 2 * HR) * breadth)
        got = jnp.dot(lhs, wide[p], preferred_element_type=jnp.float32).astype(smoothed.dtype)
        for r in range(2):
            smoothed[2 * p + r, :, rows, :] = got[:, r * breadth : (r + 1) * breadth].reshape(
                members, size, breadth
            )

    for h in range(2):
        control_loads[h].wait()

        def inner(p, carry, h=h):
            smooth(h * portion, portion, p)
            return carry

        lax.fori_loop(1, pairs - 1, inner, 0)

    def columns(c, q):
        rows = members * sizes[c]
        lhs = jnp.concatenate(
            [
                smoothed[index_ref[k, q], :, pl.ds(starts[c], sizes[c]), :].reshape(rows, breadth)
                for k in range(feeds)
            ],
            axis=1,
        )
        rhs = interp_v[q].reshape(feeds * breadth, breadth)
        spread = jnp.dot(lhs, rhs, preferred_element_type=jnp.float32)
        spread = spread.reshape(members, sizes[c], breadth)
        at = pl.ds(pl.multiple_of(q * breadth, breadth), breadth)
        return jnp.sum(perts[c][:, :, at].astype(jnp.float32) * spread, axis=0)

    def remote(src, dst, send, recv, t):
        copy = pltpu.make_async_remote_copy(
            src_ref=src, dst_ref=dst, send_sem=send, recv_sem=recv,
            device_id={"mem": flipped(t)}, device_id_type=MESH,
        )
        copy.start()
        return copy

    share = column_blocks // SIDE
    factor = 1.0 / jnp.sqrt(jnp.float32(members * mems - 1))
    reduces, exchanges, gathers, stores = {}, {}, {}, []

    def scatter(c, n, to):
        at = c * len(peers) + n
        return pltpu.make_async_remote_copy(
            src_ref=txs[c].at[n], dst_ref=rxs[c].at[n],
            send_sem=red_send.at[at], recv_sem=red_recv.at[at],
            device_id={"mem": to}, device_id_type=MESH,
        )

    def compute(c):
        for copy in halos[c]:
            copy.wait_recv()
        if c == 0:
            interp_load.wait()
        pert_loads[c].wait()
        smooth(starts[c], sizes[c], 0)
        smooth(starts[c], sizes[c], pairs - 1)
        if len(halos) < count:
            halo_left(c)
            send_halo()
        low, high = bit[0], bit[1]

        def away(n, carry):
            t = SIDE - 1 - n
            t_low, t_high = lax.rem(t, 2), t // 2
            u_low, u_high = low + t_low - 2 * low * t_low, high + t_high - 2 * high * t_high
            owner = u_low + 2 * u_high

            def one(j, inner):
                txs[c][n, j] = columns(c, owner * share + j).astype(jnp.bfloat16)
                return inner

            lax.fori_loop(0, share, one, 0, unroll=2)
            scatter(c, n, me + (u_low - low) + 2 * (u_high - high)).start()
            return carry

        lax.fori_loop(0, len(peers), away, 0)
        for n, t in enumerate(peers):
            reduces[c, n] = scatter(c, n, flipped(t))

        def kept(j, carry):
            owns[c][j] = columns(c, quarter(0) * share + j)
            return carry

        lax.fori_loop(0, share, kept, 0, unroll=2)

    def finish(c, j, total):
        at = pl.ds(j * breadth, breadth)
        finals[c][:, at] = (total * factor).astype(out_ref.dtype)

    def advance(c, stage):
        if stage == 0:
            for n in range(len(peers)):
                reduces[c, n].wait_recv()
        else:
            exchanges[c, stage - 1].wait_recv()
        for j in range(share):
            if stage == 0:
                total = owns[c][j]
                for n in range(len(peers)):
                    total = total + rxs[c][n, j].astype(jnp.float32)
            else:
                total = sums_tx[c][stage - 1][j].astype(jnp.float32) + sums_rx[c][stage - 1][
                    j
                ].astype(jnp.float32)
            if stage < later:
                sums_tx[c][stage][j] = total.astype(jnp.bfloat16)
            else:
                finish(c, j, total)
        if stage < later:
            at = c * later + stage
            exchanges[c, stage] = remote(
                sums_tx[c][stage], sums_rx[c][stage], sum_send.at[at], sum_recv.at[at], 1 << (stage + 2)
            )
            return
        place = out_ref.at[
            pl.ds(starts[c], sizes[c]),
            pl.ds(pl.multiple_of(quarter(0) * (share * breadth), breadth), share * breadth),
        ]
        for n, t in enumerate(peers):
            at = c * len(peers) + n
            gathers[c, n] = remote(finals[c], place, gat_send.at[at], gat_recv.at[at], t)
        store = pltpu.make_async_copy(finals[c], place, store_sem.at[c])
        store.start()
        stores.append(store)

    steps = [(c, 0, c, None) for c in range(count)]
    steps += [(c + 1 + stage, 1, c, stage) for c in range(count) for stage in range(later + 1)]
    for _, kind, c, stage in sorted(steps, key=lambda step: step[:3]):
        if kind == 0:
            compute(c)
        else:
            advance(c, stage)

    for c in range(max(count - 2, 0), count):
        halo_left(c)
    for group in (reduces, exchanges):
        for key in sorted(group):
            group[key].wait_send()
    for key in sorted(gathers):
        gathers[key].wait()
    for store in stores:
        store.wait()


def per_device(doms, mems, control, corr_offsets, corr_blocks, interp_index, interp_blocks, perturbations):
    members, levels, width = control.shape
    blocks, _, breadth, _ = corr_blocks.shape
    column_blocks = interp_blocks.shape[0]
    sizes = chunk_sizes(levels)
    count = len(sizes)
    later = mems.bit_length() - 3
    share = column_blocks // SIDE
    bf16, f32 = jnp.bfloat16, jnp.float32
    scratch = []
    scratch += [pltpu.VMEM((members, n, perturbations.shape[2]), bf16) for n in sizes]
    scratch += [
        pltpu.VMEM((members, levels, width + 2 * HR * breadth), bf16),
        pltpu.VMEM((blocks, members, levels, breadth), bf16),
        pltpu.VMEM(corr_blocks.shape, bf16),
        pltpu.VMEM(interp_blocks.shape, bf16),
        pltpu.VMEM((blocks // 2, (2 + 2 * HR) * breadth, 2 * breadth), bf16),
    ]
    for _ in range(2):
        scratch += [pltpu.VMEM((SIDE - 1, share, n, breadth), bf16) for n in sizes]
    for times in (later, later):
        scratch += [pltpu.VMEM((share, n, breadth), bf16) for n in sizes for _ in range(times)]
    scratch += [pltpu.VMEM((share, n, breadth), f32) for n in sizes]
    scratch += [pltpu.VMEM((n, share * breadth), bf16) for n in sizes]
    scratch += [
        pltpu.SemaphoreType.DMA((n,))
        for n in (4 + count, count, 2 * count, 2 * count, 3 * count, 3 * count)
        + (later * count, later * count, 3 * count, 3 * count)
    ]
    hbm = pl.BlockSpec(memory_space=pl.ANY)
    smem = pl.BlockSpec(memory_space=pltpu.SMEM)
    flops = 2 * members * levels * breadth * breadth * (6 * blocks + 4 * column_blocks)
    return pl.pallas_call(
        functools.partial(kernel, sizes, doms, mems),
        out_shape=jax.ShapeDtypeStruct((levels, column_blocks * breadth), bf16),
        in_specs=[smem, smem, hbm, hbm, hbm, hbm],
        out_specs=hbm,
        scratch_shapes=scratch,
        compiler_params=pltpu.CompilerParams(
            collective_id=0, has_side_effects=True, vmem_limit_bytes=56 << 20
        ),
        cost_estimate=pl.CostEstimate(flops=flops, bytes_accessed=13 << 20, transcendentals=0),
    )(corr_offsets.T, interp_index.T, control, corr_blocks, interp_blocks, perturbations)


def solution(mesh):
    in_specs = (
        P("mem", None, "dom"),
        P("dom", None),
        P("dom", None, None, None),
        P("dom", None),
        P("dom", None, None, None),
        P("mem", None, "dom"),
    )
    out_specs = P(None, "dom")
    return jax.shard_map(
        functools.partial(per_device, mesh.shape["dom"], mesh.shape["mem"]),
        mesh=mesh, in_specs=in_specs, out_specs=out_specs, check_vma=False,
    )
```

```python
import functools

import jax
import jax.numpy as jnp
from jax import lax
from jax.experimental import pallas as pl
from jax.experimental.pallas import tpu as pltpu
from jax.sharding import PartitionSpec as P

HR = 2
MESH = pl.DeviceIdType.MESH
SIDE = 4


def chunk_sizes(levels):
    if levels % 32:
        return [levels]
    return [32] * (levels // 32)


def kernel(
    sizes, doms, mems,
    offs_ref, index_ref, control_ref, corr_ref, interp_ref, pert_ref,
    out_ref,
    *scratch,
):
    count = len(sizes)
    starts = [sum(sizes[:c]) for c in range(count)]
    bits = mems.bit_length() - 1
    later = bits - 2
    peers = (3, 2, 1)
    scratch = list(scratch)

    def take(n):
        got = scratch[:n]
        del scratch[:n]
        return got

    perts = take(count)
    ext, smoothed, corr_v, interp_v, wide = take(5)
    txs, rxs = take(count), take(count)
    sums_tx = [take(later) for _ in range(count)]
    sums_rx = [take(later) for _ in range(count)]
    owns, finals = take(count), take(count)
    load_sem, store_sem, halo_send, halo_recv = take(4)
    red_send, red_recv, sum_send, sum_recv, gat_send, gat_recv = take(6)

    members = control_ref.shape[0]
    blocks, stored, breadth = corr_ref.shape[0], corr_ref.shape[1], corr_ref.shape[2]
    column_blocks, feeds = interp_ref.shape[0], interp_ref.shape[1]
    width = blocks * breadth
    edge = HR * breadth
    pairs = blocks // 2

    me_dom = lax.axis_index("dom")
    me = lax.axis_index("mem")
    right = lax.rem(me_dom + 1, doms)
    left = lax.rem(me_dom + doms - 1, doms)
    bit = [lax.rem(me // (1 << s), 2) for s in range(bits)]

    def flipped(t):
        return me + sum((1 - 2 * bit[s]) * (1 << s) for s in range(bits) if (t >> s) & 1)

    def quarter(t):
        return lax.rem(flipped(t), SIDE) if t else lax.rem(me, SIDE)

    met = list(peers) + [1 << s for s in range(2, bits)]

    def loaded(src, dst, slot):
        copy = pltpu.make_async_copy(src, dst, load_sem.at[slot])
        copy.start()
        return copy

    corr_load = loaded(corr_ref, corr_v, 0)
    barrier = pltpu.get_barrier_semaphore()
    for neighbour in (left, right):
        pl.semaphore_signal(barrier, inc=1, device_id={"dom": neighbour}, device_id_type=MESH)
    for t in met:
        pl.semaphore_signal(barrier, inc=1, device_id={"mem": flipped(t)}, device_id_type=MESH)
    pl.semaphore_wait(barrier, 2 + len(met))

    halos = []

    def send_halo():
        c = len(halos)
        if c == count:
            return
        rows = pl.ds(starts[c], sizes[c])
        pair = []
        for side, (src, dst, to) in enumerate(
            ((width - edge, 0, right), (0, edge + width, left))
        ):
            copy = pltpu.make_async_remote_copy(
                src_ref=control_ref.at[:, rows, pl.ds(src, edge)],
                dst_ref=ext.at[:, rows, pl.ds(dst, edge)],
                send_sem=halo_send.at[2 * c + side],
                recv_sem=halo_recv.at[2 * c + side],
                device_id={"dom": to},
                device_id_type=MESH,
            )
            copy.start()
            pair.append(copy)
        halos.append(pair)

    def halo_left(c):
        for copy in halos[c]:
            copy.wait_send()

    send_halo()
    portion = control_ref.shape[1] // 2
    control_loads = [
        loaded(
            control_ref.at[:, pl.ds(h * portion, portion), :],
            ext.at[:, pl.ds(h * portion, portion), pl.ds(edge, width)],
            2 + h,
        )
        for h in range(2)
    ]
    interp_load = loaded(interp_ref, interp_v, 1)
    pert_loads = [
        loaded(pert_ref.at[:, pl.ds(starts[c], sizes[c]), :], perts[c], 4 + c)
        for c in range(count)
    ]

    corr_load.wait()

    def widen(p, carry):
        for r in range(2):
            b = 2 * p + r
            for j in range(2 + 2 * HR):
                shift = j - HR - r
                cell = (
                    p,
                    pl.ds(j * breadth, breadth),
                    pl.ds(r * breadth, breadth),
                )
                if abs(shift) > HR:
                    wide[cell] = jnp.zeros((breadth, breadth), wide.dtype)
                    continue
                slot = jnp.int32(0)
                found = jnp.int32(0)
                for s in range(stored):
                    here = offs_ref[s, b] == shift
                    slot = jnp.where(here, s, slot)
                    found = jnp.where(here, 1, found)
                value = corr_v[b, slot]
                if abs(shift) == 1:
                    value = value * found.astype(jnp.float32).astype(value.dtype)
                wide[cell] = value
        return carry

    lax.fori_loop(0, pairs, widen, 0)
    send_halo()

    def smooth(start, size, p):
        rows = pl.ds(start, size)
        across = pl.ds(pl.multiple_of(2 * p * breadth, breadth), (2 + 2 * HR) * breadth)
        lhs = ext[:, rows, across].reshape(members * size, (2 + 2 * HR) * breadth)
        got = jnp.dot(lhs, wide[p], preferred_element_type=jnp.float32).astype(smoothed.dtype)
        for r in range(2):
            smoothed[2 * p + r, :, rows, :] = got[:, r * breadth : (r + 1) * breadth].reshape(
                members, size, breadth
            )

    for h in range(2):
        control_loads[h].wait()

        def inner(p, carry, h=h):
            smooth(h * portion, portion, p)
            return carry

        lax.fori_loop(1, pairs - 1, inner, 0)

    def columns(c, q):
        rows = members * sizes[c]
        lhs = jnp.concatenate(
            [
                smoothed[index_ref[k, q], :, pl.ds(starts[c], sizes[c]), :].reshape(rows, breadth)
                for k in range(feeds)
            ],
            axis=1,
        )
        rhs = interp_v[q].reshape(feeds * breadth, breadth)
        spread = jnp.dot(lhs, rhs, preferred_element_type=jnp.float32)
        spread = spread.reshape(members, sizes[c], breadth)
        at = pl.ds(pl.multiple_of(q * breadth, breadth), breadth)
        return jnp.sum(perts[c][:, :, at].astype(jnp.float32) * spread, axis=0)

    def remote(src, dst, send, recv, t):
        copy = pltpu.make_async_remote_copy(
            src_ref=src, dst_ref=dst, send_sem=send, recv_sem=recv,
            device_id={"mem": flipped(t)}, device_id_type=MESH,
        )
        copy.start()
        return copy

    share = column_blocks // SIDE
    factor = 1.0 / jnp.sqrt(jnp.float32(members * mems - 1))
    reduces, exchanges, gathers, stores = {}, {}, {}, []

    def scatter(c, n, to):
        at = c * len(peers) + n
        return pltpu.make_async_remote_copy(
            src_ref=txs[c].at[n], dst_ref=rxs[c].at[n],
            send_sem=red_send.at[at], recv_sem=red_recv.at[at],
            device_id={"mem": to}, device_id_type=MESH,
        )

    def compute(c):
        for copy in halos[c]:
            copy.wait_recv()
        if c == 0:
            interp_load.wait()
        pert_loads[c].wait()
        smooth(starts[c], sizes[c], 0)
        smooth(starts[c], sizes[c], pairs - 1)
        if len(halos) < count:
            halo_left(c)
            send_halo()
        low, high = bit[0], bit[1]

        def away(n, carry):
            t = SIDE - 1 - n
            t_low, t_high = lax.rem(t, 2), t // 2
            u_low, u_high = low + t_low - 2 * low * t_low, high + t_high - 2 * high * t_high
            owner = u_low + 2 * u_high

            def one(j, inner):
                txs[c][n, j] = columns(c, owner * share + j).astype(jnp.bfloat16)
                return inner

            lax.fori_loop(0, share, one, 0, unroll=2)
            scatter(c, n, me + (u_low - low) + 2 * (u_high - high)).start()
            return carry

        lax.fori_loop(0, len(peers), away, 0)
        for n, t in enumerate(peers):
            reduces[c, n] = scatter(c, n, flipped(t))

        def kept(j, carry):
            owns[c][j] = columns(c, quarter(0) * share + j)
            return carry

        lax.fori_loop(0, share, kept, 0, unroll=2)

    def finish(c, j, total):
        at = pl.ds(j * breadth, breadth)
        finals[c][:, at] = (total * factor).astype(out_ref.dtype)

    def advance(c, stage):
        if stage == 0:
            for n in range(len(peers)):
                reduces[c, n].wait_recv()
        else:
            exchanges[c, stage - 1].wait_recv()
        for j in range(share):
            if stage == 0:
                total = owns[c][j]
                for n in range(len(peers)):
                    total = total + rxs[c][n, j].astype(jnp.float32)
            else:
                total = sums_tx[c][stage - 1][j].astype(jnp.float32) + sums_rx[c][stage - 1][
                    j
                ].astype(jnp.float32)
            if stage < later:
                sums_tx[c][stage][j] = total.astype(jnp.bfloat16)
            else:
                finish(c, j, total)
        if stage < later:
            at = c * later + stage
            exchanges[c, stage] = remote(
                sums_tx[c][stage], sums_rx[c][stage], sum_send.at[at], sum_recv.at[at], 1 << (stage + 2)
            )
            return
        place = out_ref.at[
            pl.ds(starts[c], sizes[c]),
            pl.ds(pl.multiple_of(quarter(0) * (share * breadth), breadth), share * breadth),
        ]
        for n, t in enumerate(peers):
            at = c * len(peers) + n
            gathers[c, n] = remote(finals[c], place, gat_send.at[at], gat_recv.at[at], t)
        store = pltpu.make_async_copy(finals[c], place, store_sem.at[c])
        store.start()
        stores.append(store)

    steps = [(c, 0, c, None) for c in range(count)]
    steps += [(c + 1 + stage, 1, c, stage) for c in range(count) for stage in range(later + 1)]
    for _, kind, c, stage in sorted(steps, key=lambda step: step[:3]):
        if kind == 0:
            compute(c)
        else:
            advance(c, stage)

    for c in range(max(count - 2, 0), count):
        halo_left(c)
    for group in (reduces, exchanges):
        for key in sorted(group):
            group[key].wait_send()
    for key in sorted(gathers):
        gathers[key].wait()
    for store in stores:
        store.wait()


def per_device(doms, mems, control, corr_offsets, corr_blocks, interp_index, interp_blocks, perturbations):
    members, levels, width = control.shape
    blocks, _, breadth, _ = corr_blocks.shape
    column_blocks = interp_blocks.shape[0]
    sizes = chunk_sizes(levels)
    count = len(sizes)
    later = mems.bit_length() - 3
    share = column_blocks // SIDE
    bf16, f32 = jnp.bfloat16, jnp.float32
    scratch = []
    scratch += [pltpu.VMEM((members, n, perturbations.shape[2]), bf16) for n in sizes]
    scratch += [
        pltpu.VMEM((members, levels, width + 2 * HR * breadth), bf16),
        pltpu.VMEM((blocks, members, levels, breadth), bf16),
        pltpu.VMEM(corr_blocks.shape, bf16),
        pltpu.VMEM(interp_blocks.shape, bf16),
        pltpu.VMEM((blocks // 2, (2 + 2 * HR) * breadth, 2 * breadth), bf16),
    ]
    for _ in range(2):
        scratch += [pltpu.VMEM((SIDE - 1, share, n, breadth), bf16) for n in sizes]
    for times in (later, later):
        scratch += [pltpu.VMEM((share, n, breadth), bf16) for n in sizes for _ in range(times)]
    scratch += [pltpu.VMEM((share, n, breadth), f32) for n in sizes]
    scratch += [pltpu.VMEM((n, share * breadth), bf16) for n in sizes]
    scratch += [
        pltpu.SemaphoreType.DMA((n,))
        for n in (4 + count, count, 2 * count, 2 * count, 3 * count, 3 * count)
        + (later * count, later * count, 3 * count, 3 * count)
    ]
    hbm = pl.BlockSpec(memory_space=pl.ANY)
    smem = pl.BlockSpec(memory_space=pltpu.SMEM)
    flops = 2 * members * levels * breadth * breadth * (6 * blocks + 4 * column_blocks)
    return pl.pallas_call(
        functools.partial(kernel, sizes, doms, mems),
        out_shape=jax.ShapeDtypeStruct((levels, column_blocks * breadth), bf16),
        in_specs=[smem, smem, hbm, hbm, hbm, hbm],
        out_specs=hbm,
        scratch_shapes=scratch,
        compiler_params=pltpu.CompilerParams(
            collective_id=0, has_side_effects=True, vmem_limit_bytes=56 << 20
        ),
        cost_estimate=pl.CostEstimate(flops=flops, bytes_accessed=13 << 20, transcendentals=0),
    )(corr_offsets.T, interp_index.T, control, corr_blocks, interp_blocks, perturbations)


def solution(mesh):
    in_specs = (
        P("mem", None, "dom"),
        P("dom", None),
        P("dom", None, None, None),
        P("dom", None),
        P("dom", None, None, None),
        P("mem", None, "dom"),
    )
    out_specs = P(None, "dom")
    return jax.shard_map(
        functools.partial(per_device, mesh.shape["dom"], mesh.shape["mem"]),
        mesh=mesh, in_specs=in_specs, out_specs=out_specs, check_vma=False,
    )
```

```python
import functools

import jax
import jax.numpy as jnp
from jax import lax
from jax.experimental import pallas as pl
from jax.experimental.pallas import tpu as pltpu
from jax.sharding import PartitionSpec as P

HR = 2
MESH = pl.DeviceIdType.MESH
SIDE = 4


def chunk_sizes(levels):
    if levels % 32:
        return [levels]
    return [32] * (levels // 32 - 1) + [16, 16]


def kernel(
    sizes, doms, mems,
    offs_ref, index_ref, control_ref, corr_ref, interp_ref, pert_ref,
    out_ref,
    *scratch,
):
    count = len(sizes)
    starts = [sum(sizes[:c]) for c in range(count)]
    bits = mems.bit_length() - 1
    later = bits - 2
    peers = (3, 2, 1)
    scratch = list(scratch)

    def take(n):
        got = scratch[:n]
        del scratch[:n]
        return got

    perts = take(count)
    ext, smoothed, corr_v, interp_v, wide = take(5)
    txs, rxs = take(count), take(count)
    sums_tx = [take(later) for _ in range(count)]
    sums_rx = [take(later) for _ in range(count)]
    owns, finals = take(count), take(count)
    load_sem, store_sem, halo_send, halo_recv = take(4)
    red_send, red_recv, sum_send, sum_recv, gat_send, gat_recv = take(6)

    members = control_ref.shape[0]
    blocks, stored, breadth = corr_ref.shape[0], corr_ref.shape[1], corr_ref.shape[2]
    column_blocks, feeds = interp_ref.shape[0], interp_ref.shape[1]
    width = blocks * breadth
    edge = HR * breadth
    pairs = blocks // 2

    me_dom = lax.axis_index("dom")
    me = lax.axis_index("mem")
    right = lax.rem(me_dom + 1, doms)
    left = lax.rem(me_dom + doms - 1, doms)
    bit = [lax.rem(me // (1 << s), 2) for s in range(bits)]

    def flipped(t):
        return me + sum((1 - 2 * bit[s]) * (1 << s) for s in range(bits) if (t >> s) & 1)

    def quarter(t):
        return lax.rem(flipped(t), SIDE) if t else lax.rem(me, SIDE)

    met = list(peers) + [1 << s for s in range(2, bits)]

    def loaded(src, dst, slot):
        copy = pltpu.make_async_copy(src, dst, load_sem.at[slot])
        copy.start()
        return copy

    corr_load = loaded(corr_ref, corr_v, 0)
    barrier = pltpu.get_barrier_semaphore()
    for neighbour in (left, right):
        pl.semaphore_signal(barrier, inc=1, device_id={"dom": neighbour}, device_id_type=MESH)
    for t in met:
        pl.semaphore_signal(barrier, inc=1, device_id={"mem": flipped(t)}, device_id_type=MESH)
    pl.semaphore_wait(barrier, 2 + len(met))

    halos = []

    def send_halo():
        c = len(halos)
        if c == count:
            return
        rows = pl.ds(starts[c], sizes[c])
        pair = []
        for side, (src, dst, to) in enumerate(
            ((width - edge, 0, right), (0, edge + width, left))
        ):
            copy = pltpu.make_async_remote_copy(
                src_ref=control_ref.at[:, rows, pl.ds(src, edge)],
                dst_ref=ext.at[:, rows, pl.ds(dst, edge)],
                send_sem=halo_send.at[2 * c + side],
                recv_sem=halo_recv.at[2 * c + side],
                device_id={"dom": to},
                device_id_type=MESH,
            )
            copy.start()
            pair.append(copy)
        halos.append(pair)

    def halo_left(c):
        for copy in halos[c]:
            copy.wait_send()

    send_halo()
    portion = control_ref.shape[1] // 2
    control_loads = [
        loaded(
            control_ref.at[:, pl.ds(h * portion, portion), :],
            ext.at[:, pl.ds(h * portion, portion), pl.ds(edge, width)],
            2 + h,
        )
        for h in range(2)
    ]
    interp_load = loaded(interp_ref, interp_v, 1)
    pert_loads = [
        loaded(pert_ref.at[:, pl.ds(starts[c], sizes[c]), :], perts[c], 4 + c)
        for c in range(count)
    ]

    corr_load.wait()

    def widen(p, carry):
        for r in range(2):
            b = 2 * p + r
            for j in range(2 + 2 * HR):
                shift = j - HR - r
                cell = (
                    p,
                    pl.ds(j * breadth, breadth),
                    pl.ds(r * breadth, breadth),
                )
                if abs(shift) > HR:
                    wide[cell] = jnp.zeros((breadth, breadth), wide.dtype)
                    continue
                slot = jnp.int32(0)
                found = jnp.int32(0)
                for s in range(stored):
                    here = offs_ref[s, b] == shift
                    slot = jnp.where(here, s, slot)
                    found = jnp.where(here, 1, found)
                value = corr_v[b, slot]
                if abs(shift) == 1:
                    value = value * found.astype(jnp.float32).astype(value.dtype)
                wide[cell] = value
        return carry

    lax.fori_loop(0, pairs, widen, 0)
    send_halo()

    def smooth(start, size, p):
        rows = pl.ds(start, size)
        across = pl.ds(pl.multiple_of(2 * p * breadth, breadth), (2 + 2 * HR) * breadth)
        lhs = ext[:, rows, across].reshape(members * size, (2 + 2 * HR) * breadth)
        got = jnp.dot(lhs, wide[p], preferred_element_type=jnp.float32).astype(smoothed.dtype)
        for r in range(2):
            smoothed[2 * p + r, :, rows, :] = got[:, r * breadth : (r + 1) * breadth].reshape(
                members, size, breadth
            )

    for h in range(2):
        control_loads[h].wait()

        def inner(p, carry, h=h):
            smooth(h * portion, portion, p)
            return carry

        lax.fori_loop(1, pairs - 1, inner, 0)
        send_halo()

    while len(halos) < count:
        send_halo()

    def columns(c, q):
        rows = members * sizes[c]
        lhs = jnp.concatenate(
            [
                smoothed[index_ref[k, q], :, pl.ds(starts[c], sizes[c]), :].reshape(rows, breadth)
                for k in range(feeds)
            ],
            axis=1,
        )
        rhs = interp_v[q].reshape(feeds * breadth, breadth)
        spread = jnp.dot(lhs, rhs, preferred_element_type=jnp.float32)
        spread = spread.reshape(members, sizes[c], breadth)
        at = pl.ds(pl.multiple_of(q * breadth, breadth), breadth)
        return jnp.sum(perts[c][:, :, at].astype(jnp.float32) * spread, axis=0)

    def remote(src, dst, send, recv, t):
        copy = pltpu.make_async_remote_copy(
            src_ref=src, dst_ref=dst, send_sem=send, recv_sem=recv,
            device_id={"mem": flipped(t)}, device_id_type=MESH,
        )
        copy.start()
        return copy

    share = column_blocks // SIDE
    factor = 1.0 / jnp.sqrt(jnp.float32(members * mems - 1))
    reduces, exchanges, gathers, stores = {}, {}, {}, []

    def scatter(c, n, to):
        at = c * len(peers) + n
        return pltpu.make_async_remote_copy(
            src_ref=txs[c].at[n], dst_ref=rxs[c].at[n],
            send_sem=red_send.at[at], recv_sem=red_recv.at[at],
            device_id={"mem": to}, device_id_type=MESH,
        )

    def compute(c):
        for copy in halos[c]:
            copy.wait_recv()
        if c == 0:
            interp_load.wait()
        pert_loads[c].wait()
        smooth(starts[c], sizes[c], 0)
        smooth(starts[c], sizes[c], pairs - 1)
        low, high = bit[0], bit[1]

        def away(n, carry):
            t = SIDE - 1 - n
            t_low, t_high = lax.rem(t, 2), t // 2
            u_low, u_high = low + t_low - 2 * low * t_low, high + t_high - 2 * high * t_high
            owner = u_low + 2 * u_high

            def one(j, inner):
                txs[c][n, j] = columns(c, owner * share + j).astype(jnp.bfloat16)
                return inner

            lax.fori_loop(0, share, one, 0, unroll=2)
            scatter(c, n, me + (u_low - low) + 2 * (u_high - high)).start()
            return carry

        lax.fori_loop(0, len(peers), away, 0)
        for n, t in enumerate(peers):
            reduces[c, n] = scatter(c, n, flipped(t))

        def kept(j, carry):
            owns[c][j] = columns(c, quarter(0) * share + j)
            return carry

        lax.fori_loop(0, share, kept, 0, unroll=2)

    def finish(c, j, total):
        at = pl.ds(j * breadth, breadth)
        finals[c][:, at] = (total * factor).astype(out_ref.dtype)

    def advance(c, stage):
        if stage == 0:
            for n in range(len(peers)):
                reduces[c, n].wait_recv()
        else:
            exchanges[c, stage - 1].wait_recv()
        for j in range(share):
            if stage == 0:
                total = owns[c][j]
                for n in range(len(peers)):
                    total = total + rxs[c][n, j].astype(jnp.float32)
            else:
                total = sums_tx[c][stage - 1][j].astype(jnp.float32) + sums_rx[c][stage - 1][
                    j
                ].astype(jnp.float32)
            if stage < later:
                sums_tx[c][stage][j] = total.astype(jnp.bfloat16)
            else:
                finish(c, j, total)
        if stage < later:
            at = c * later + stage
            exchanges[c, stage] = remote(
                sums_tx[c][stage], sums_rx[c][stage], sum_send.at[at], sum_recv.at[at], 1 << (stage + 2)
            )
            return
        place = out_ref.at[
            pl.ds(starts[c], sizes[c]),
            pl.ds(pl.multiple_of(quarter(0) * (share * breadth), breadth), share * breadth),
        ]
        for n, t in enumerate(peers):
            at = c * len(peers) + n
            gathers[c, n] = remote(finals[c], place, gat_send.at[at], gat_recv.at[at], t)
        store = pltpu.make_async_copy(finals[c], place, store_sem.at[c])
        store.start()
        stores.append(store)

    steps = [(c, 0, c, None) for c in range(count)]
    steps += [(c + 1 + stage, 1, c, stage) for c in range(count) for stage in range(later + 1)]
    for _, kind, c, stage in sorted(steps, key=lambda step: step[:3]):
        if kind == 0:
            compute(c)
        else:
            advance(c, stage)

    for c in range(count):
        halo_left(c)
    for group in (reduces, exchanges):
        for key in sorted(group):
            group[key].wait_send()
    for key in sorted(gathers):
        gathers[key].wait()
    for store in stores:
        store.wait()


def per_device(doms, mems, control, corr_offsets, corr_blocks, interp_index, interp_blocks, perturbations):
    members, levels, width = control.shape
    blocks, _, breadth, _ = corr_blocks.shape
    column_blocks = interp_blocks.shape[0]
    sizes = chunk_sizes(levels)
    count = len(sizes)
    later = mems.bit_length() - 3
    share = column_blocks // SIDE
    bf16, f32 = jnp.bfloat16, jnp.float32
    scratch = []
    scratch += [pltpu.VMEM((members, n, perturbations.shape[2]), bf16) for n in sizes]
    scratch += [
        pltpu.VMEM((members, levels, width + 2 * HR * breadth), bf16),
        pltpu.VMEM((blocks, members, levels, breadth), bf16),
        pltpu.VMEM(corr_blocks.shape, bf16),
        pltpu.VMEM(interp_blocks.shape, bf16),
        pltpu.VMEM((blocks // 2, (2 + 2 * HR) * breadth, 2 * breadth), bf16),
    ]
    for _ in range(2):
        scratch += [pltpu.VMEM((SIDE - 1, share, n, breadth), bf16) for n in sizes]
    for times in (later, later):
        scratch += [pltpu.VMEM((share, n, breadth), bf16) for n in sizes for _ in range(times)]
    scratch += [pltpu.VMEM((share, n, breadth), f32) for n in sizes]
    scratch += [pltpu.VMEM((n, share * breadth), bf16) for n in sizes]
    scratch += [
        pltpu.SemaphoreType.DMA((n,))
        for n in (4 + count, count, 2 * count, 2 * count, 3 * count, 3 * count)
        + (later * count, later * count, 3 * count, 3 * count)
    ]
    hbm = pl.BlockSpec(memory_space=pl.ANY)
    smem = pl.BlockSpec(memory_space=pltpu.SMEM)
    flops = 2 * members * levels * breadth * breadth * (6 * blocks + 4 * column_blocks)
    return pl.pallas_call(
        functools.partial(kernel, sizes, doms, mems),
        out_shape=jax.ShapeDtypeStruct((levels, column_blocks * breadth), bf16),
        in_specs=[smem, smem, hbm, hbm, hbm, hbm],
        out_specs=hbm,
        scratch_shapes=scratch,
        compiler_params=pltpu.CompilerParams(
            collective_id=0, has_side_effects=True, vmem_limit_bytes=56 << 20
        ),
        cost_estimate=pl.CostEstimate(flops=flops, bytes_accessed=13 << 20, transcendentals=0),
    )(corr_offsets.T, interp_index.T, control, corr_blocks, interp_blocks, perturbations)


def solution(mesh):
    in_specs = (
        P("mem", None, "dom"),
        P("dom", None),
        P("dom", None, None, None),
        P("dom", None),
        P("dom", None, None, None),
        P("mem", None, "dom"),
    )
    out_specs = P(None, "dom")
    return jax.shard_map(
        functools.partial(per_device, mesh.shape["dom"], mesh.shape["mem"]),
        mesh=mesh, in_specs=in_specs, out_specs=out_specs, check_vma=False,
    )
```
